32 devices in a mesh: gx: 4 (over y, x), gz: 2 (over core), ta: 4 (over z).
Axes of the slice: x: 2, y: 2, z: 4, core: 2. Of those that a mesh axis runs over, the one named last changes fastest.
Arguments:
- right_side: float32 [512, 64, 128], P(('gx', 'ta'), 'gz'), may hold values from -8 to 8
- diagonal: float32 [512, 64, 128], P(('gx', 'ta'), 'gz'), may hold values from 0.05 to 1
- coupling: float32 [128, 128], replicated, as said below
- wall_owner: int32 [2048, 1], P(('gx', 'gz', 'ta')), may hold values from 0 to 15; in each aligned block of 64 rows (0 to 63, 64 to 127, ...) at most 8 rows name the same one
- neighbours: int32 [2048, 4], P(('gx', 'gz', 'ta')), may hold values from 0 to 63
- input_weight: bfloat16 [256, 128], replicated, may hold values from -0.375 to 0.375
- head_weights: bfloat16 [16, 128, 128], P(('gx', 'ta')), may hold values from -0.5 to 0.5
- output_weight: float32 [128], replicated, may hold values from -0.5 to 0.5
Outputs:
- solution_field: float32 [512, 64, 128], P(('gx', 'ta'), 'gz')
- residual: float32 [512, 64, 128], P(('gx', 'ta'), 'gz')
- input_grad: float32 [256, 128], replicated
- head_grad: float32 [16, 128, 128], P(('gx', 'ta'))
- output_grad: float32 [128], replicated
The draws below stay inside these ranges and needn't reach their ends.
Inputs may be any that keep to these rules, and one draw needn't show every extreme that they name: `wall_owner`: among the wall elements of one device, no trainer is named more than 8 times, a bound that some block reaches. `neighbours`: each entry is a local element number of the element's own device. `coupling`: Symmetric; diagonal entries between 0.4 and 1.4; off-diagonal entries of magnitude at most 0.25 / sqrt(128).
All inputs are finite; a program needn't handle non-finite values.
Results may differ from the reference program's by a relative error of at most 0.004.
Values may be sent and summed in bfloat16 or wider, within the bound.
A program may use at most 64 MiB of HBM per device.

```python
import math
import jax
import jax.numpy as jnp
import numpy as np
from jax import lax

CX = 32
CZ = 32
NY = 128
HID = 128
EL = 4
ITERS = 6
TRAIN = 16
E_DEV = 64
CAP = 8
ELEMS = 2048
NX = 512
NZ = 64
N_GX = 4
N_GZ = 2
N_TA = 4


def draw_coupling(key, part):
    key = jax.random.fold_in(key, 11)
    random_part = jax.random.uniform(jax.random.fold_in(key, 1), (NY, NY), jnp.float32, -1.0, 1.0)
    diagonal_part = jax.random.uniform(jax.random.fold_in(key, 2), (NY,), jnp.float32, 0.4, 1.4)
    symmetric = 0.5 * (random_part + random_part.T) * (0.25 / jnp.sqrt(jnp.float32(NY)))
    identity = jnp.eye(NY, dtype=jnp.float32)
    return symmetric * (1.0 - identity) + identity * diagonal_part[None, :]


def draw_right_side(key, part):
    key = jax.random.fold_in(key, 23)
    phases = jax.random.uniform(jax.random.fold_in(key, 1), (4,), jnp.float32, -math.pi, math.pi)
    profile = jax.random.uniform(jax.random.fold_in(key, 2), (NY,), jnp.float32, 0.5, 1.5)
    first = jnp.arange(NX).astype(jnp.float32) * (2.0 * math.pi / NX)
    second = jnp.arange(NZ).astype(jnp.float32) * (2.0 * math.pi / NZ)
    wave = 1.2 * jnp.cos(first + phases[0])[:, None] + 0.8 * jnp.cos(second + phases[1])[None, :]
    wave = wave + 0.8 * jnp.cos(first + phases[2])[:, None] * jnp.cos(second + phases[3])[None, :]
    noise = jax.random.normal(jax.random.fold_in(key, 3), (NX, NZ, NY), jnp.float32)
    smooth = wave
    return jnp.clip(noise + smooth[:, :, None] * profile[None, None, :], -8.0, 8.0)


def with_ends(values, own_key, least, top_value):
    longest = values.shape.index(max(values.shape))
    spots = []
    for shift in (0, 1):
        where = [jax.random.randint(jax.random.fold_in(own_key, axis), (), 0, length) for axis, length in enumerate(values.shape)]
        where[longest] = (where[longest] + shift) % values.shape[longest]
        spots.append(tuple(where))
    return values.at[spots[0]].set(least).at[spots[1]].set(top_value)


def block_levels(rng, shape, cuts, smallest, high):
    level, own = 1.0, jax.random.fold_in(rng, 6)
    for axis_at, blocks in cuts:
        draws = jnp.exp(jax.random.uniform(jax.random.fold_in(own, axis_at), (blocks,), jnp.float32, smallest / len(cuts), high / len(cuts)))
        level = level * jnp.repeat(draws, shape[axis_at] // blocks).reshape([-1 if axis == axis_at else 1 for axis in range(len(shape))])
    return level


def routed_block(key, own, number, rows, number_of, top, limit, slope):
    sequence = jax.random.permutation(key, number_of)
    crowded, ordinary = portions_of(number_of, rows * top, limit, slope, True), portions_of(number_of, rows * top, limit, slope, False)
    places = jnp.arange(number_of)

    def named(tallies, offset_by):
        used = int((tallies > 0).sum())
        fixed = max(1, used // 4)
        shifted = fixed + (places - fixed + offset_by * (used - fixed)) % max(1, number_of - fixed)
        return jnp.zeros((number_of,), jnp.int32).at[sequence[jnp.where(places < fixed, places, shifted)]].set(jnp.asarray(tallies, jnp.int32))

    tallies = jnp.where(number % 4 == 0, named(crowded, number // 4), named(ordinary, number - number // 4 - 1))
    mixed = jax.random.permutation(jax.random.fold_in(own, 3), number_of)
    giver, sink = mixed[0:number_of // 2 * 2:2], mixed[1:number_of // 2 * 2:2]
    margin = jnp.minimum(tallies[giver] - 1, limit - tallies[sink]) // 2
    margin = jnp.where((giver == sequence[0]) | (sink == sequence[0]) | (tallies[sink] == 0), 0, jnp.maximum(margin, 0))
    shifted = jax.random.randint(jax.random.fold_in(own, 4), (number_of // 2,), 0, 1 << 20) % (margin + 1)
    tallies = tallies.at[giver].add(-shifted).at[sink].add(shifted)
    members = jnp.searchsorted(jnp.cumsum(tallies), jnp.arange(rows * top), side="right").astype(jnp.int32)
    table = members.reshape(top, rows).T
    table = table[jax.random.permutation(jax.random.fold_in(own, 1), rows)]
    offset_by = jax.random.randint(jax.random.fold_in(own, 2), (rows, 1), 0, top)
    return jnp.take_along_axis(table, (jnp.arange(top)[None, :] + offset_by) % top, axis=1)


def portions_of(amount, total, most, skew, full):
    portions = [(1 << 20) // math.isqrt(standing ** skew) + 1 for standing in range(1, amount + 1)]
    largest = most if full else min(most, max(-(-total // amount), total * portions[0] // sum(portions)))
    least = 1 if total - largest >= amount - 1 else 0
    counts, surplus = [largest] + [least] * (amount - 1), total - largest - least * (amount - 1)
    while surplus > 0:
        free = [i for i in range(1, amount) if counts[i] < largest] or [i for i in range(1, amount) if counts[i] < most]
        mass, remaining = sum([portions[i] for i in free]), surplus
        for i in free:
            more = min(most - counts[i], max(1, remaining * portions[i] // mass), surplus)
            counts[i] = counts[i] + more
            surplus = surplus - more
    return np.array(counts)


def gaussian(stream_key, dims, deviation, bound, cuts=(), kind=jnp.bfloat16):
    result = deviation * jax.random.normal(stream_key, dims, jnp.float32)
    if cuts:
        result = result * block_levels(stream_key, dims, cuts, -0.22, 0.18)
    return jnp.clip(result, -bound, bound).astype(kind)


def setup_inputs(seed: int = 0) -> dict:
    seeds = jax.random.split(jax.random.key(seed), 9)
    right_side = draw_right_side(jax.random.fold_in(seeds[8], 71), 0)
    diagonal = jnp.clip(jnp.exp(math.log(1.0) - 2.9957323 * jax.random.uniform(seeds[1], (NX, NZ, NY), jnp.float32) ** block_levels(seeds[1], (NX, NZ, NY), ((0, 16), (1, 2)), -0.2, 0.2)), 0.05, 1.0)
    coupling = draw_coupling(jax.random.fold_in(seeds[8], 71), 0)
    wall_owner_keys = jax.random.split(jax.random.fold_in(seeds[3], 1), ELEMS // E_DEV)
    wall_owner_turns = jax.random.permutation(jax.random.fold_in(seeds[3], 3), ELEMS // E_DEV)
    wall_owner = jax.vmap(lambda own, number: routed_block(jax.random.fold_in(seeds[3], 2), own, number, E_DEV, TRAIN, 1, CAP, 2))(wall_owner_keys, wall_owner_turns).reshape((ELEMS, 1))
    neighbours = with_ends(jax.random.randint(seeds[4], (ELEMS, 4), 0, E_DEV), jax.random.fold_in(seeds[4], 1), 0, E_DEV - 1).astype(jnp.int32)
    input_weight = gaussian(seeds[5], (2 * NY, HID), (2 * NY) ** -0.5, 0.375)
    head_weights = gaussian(seeds[6], (TRAIN, HID, HID), HID ** -0.5, 0.5, ((0, 16),))
    output_weight = gaussian(seeds[7], (HID,), HID ** -0.5, 0.5, (), jnp.float32)
    return {"right_side": right_side, "diagonal": diagonal, "coupling": coupling, "wall_owner": wall_owner, "neighbours": neighbours, "input_weight": input_weight, "head_weights": head_weights, "output_weight": output_weight}


def silu_slope(inputs):
    sigmoid_val = jax.nn.sigmoid(inputs)
    return sigmoid_val * (1.0 + inputs * (1.0 - sigmoid_val))


def operate(grid_field, diagonal, coupling):
    beside = jnp.roll(grid_field, 1, 0) + jnp.roll(grid_field, -1, 0)
    beside = beside + jnp.roll(grid_field, 1, 1) + jnp.roll(grid_field, -1, 1)
    normal_part = jnp.dot(grid_field.reshape(-1, NY), coupling, precision=lax.Precision.HIGHEST).reshape(grid_field.shape)
    return (4.0 + diagonal) * grid_field - beside + normal_part


def pool(grid_vals):
    trailing = grid_vals.shape[2:]
    shaped = grid_vals.reshape((NX // EL, EL, NZ // EL, EL) + trailing)
    return jnp.sum(shaped, axis=(1, 3)) / EL


def by_device(blocks):
    trailing = blocks.shape[2:]
    shaped = blocks.reshape((N_GX, N_TA, CX // EL, N_GZ, CZ // EL) + trailing)
    permuted_axes = (0, 3, 1, 2, 4) + tuple(range(5, 5 + len(trailing)))
    return jnp.transpose(shaped, permuted_axes).reshape((N_GX * N_GZ * N_TA * E_DEV,) + trailing)


def reference(right_side, diagonal, coupling, wall_owner, neighbours, input_weight, head_weights, output_weight):
    solution_field = jnp.zeros_like(right_side)
    residual = right_side
    direction = right_side
    norm_now = jnp.sum(residual * residual)
    for iteration in range(ITERS):
        applied = operate(direction, diagonal, coupling)
        step_size = norm_now / jnp.sum(direction * applied)
        solution_field = solution_field + step_size * direction
        residual = residual - step_size * applied
        norm_next = jnp.sum(residual * residual)
        direction = residual + (norm_next / norm_now) * direction
        norm_now = norm_next
    wall_feat = by_device(pool(solution_field)).astype(jnp.bfloat16)
    wall_shear = by_device(pool(solution_field[:, :, 1] - solution_field[:, :, 0])).astype(jnp.bfloat16)
    samples = wall_feat.shape[0]
    per_device = wall_feat.reshape(-1, E_DEV, NY).astype(jnp.float32)
    local_ids = neighbours.reshape(-1, E_DEV, 4)
    gathered = jax.vmap(lambda table, rows: table[rows])(per_device, local_ids)
    graph_mean = jnp.mean(gathered, axis=2).reshape(samples, NY).astype(jnp.bfloat16)
    node_input = jnp.concatenate([wall_feat, graph_mean], axis=1)
    preact = jnp.dot(node_input, input_weight, preferred_element_type=jnp.float32)
    hidden = jax.nn.silu(preact).astype(jnp.bfloat16)
    owners = wall_owner[:, 0]
    trainers = head_weights.shape[0]
    width = math.gcd(512, samples)

    def one_block(carry, block):
        hidden_blk, shear_blk, owner_blk = block
        chosen = head_weights[owner_blk].astype(jnp.float32)
        head_pre = jnp.einsum('bk,bkl->bl', hidden_blk.astype(jnp.float32), chosen)
        head_out = jax.nn.silu(head_pre)
        predicted = jnp.sum(head_out * output_weight, axis=1)
        misfit = (predicted - shear_blk.astype(jnp.float32)) / E_DEV
        head_back = (misfit[:, None] * output_weight * silu_slope(head_pre)).astype(jnp.bfloat16)
        owner_hits = (owner_blk[:, None] == jnp.arange(trainers, dtype=jnp.int32)[None, :]).astype(jnp.float32)
        outer_prod = jnp.einsum('bk,bl->bkl', hidden_blk.astype(jnp.float32), head_back.astype(jnp.float32))
        head_sum = carry[0] + jnp.einsum('be,bkl->ekl', owner_hits, outer_prod)
        out_sum = carry[1] + jnp.sum(misfit[:, None] * head_out, axis=0)
        hidden_back = jnp.einsum('bl,bkl->bk', head_back.astype(jnp.float32), chosen).astype(jnp.bfloat16)
        return (head_sum, out_sum), hidden_back

    start = (jnp.zeros((trainers, HID, HID), jnp.float32), jnp.zeros((HID,), jnp.float32))
    blocks = (hidden.reshape(-1, width, HID), wall_shear.reshape(-1, width), owners.reshape(-1, width))
    (head_grad, output_grad), hidden_back = lax.scan(one_block, start, blocks)
    hidden_back = hidden_back.reshape(samples, HID)
    preact_back = (hidden_back.astype(jnp.float32) * silu_slope(preact)).astype(jnp.bfloat16)
    input_grad = jnp.dot(node_input.T, preact_back, preferred_element_type=jnp.float32)
    return solution_field, residual, input_grad, head_grad, output_grad
```

```python
import functools
import jax
import jax.numpy as jnp
from jax import lax
from jax.experimental import pallas as pl
from jax.experimental.pallas import tpu as pltpu
from jax.sharding import PartitionSpec as P

EL = 4
ITERS = 6
HX = ITERS
HZ = 8
CENTRE = 5.3
SPREAD = 5.4
PLANES = 14
MESH = pl.DeviceIdType.MESH
F32 = jnp.float32
BF16 = jnp.bfloat16

DIRS = [(dx, dz) for dx in (-1, 0, 1) for dz in (-1, 0, 1) if (dx, dz) != (0, 0)]


def tree_sum(terms):
    terms = list(terms)
    while len(terms) > 1:
        terms = [
            terms[i] + terms[i + 1] if i + 1 < len(terms) else terms[i]
            for i in range(0, len(terms), 2)
        ]
    return terms[0]


def sigmoid(v):
    return 1.0 / (1.0 + jnp.exp(-v))


def dot_rows(a, b):
    return lax.dot_general(a, b, (((0,), (0,)), ((), ())), preferred_element_type=F32)


def dot_lanes(a, b):
    return lax.dot_general(a, b, (((1,), (1,)), ((), ())), preferred_element_type=F32)


def kernel(
    sizes,
    rhs_hbm,
    diag_hbm,
    coup_ref,
    owner_ref,
    neigh_ref,
    w_in_ref,
    head_ref,
    w_out_ref,
    x_ref,
    r_ref,
    ig_ref,
    hg_ref,
    og_ref,
    basis,
    diag,
    heads,
    c_split,
    gram_send,
    gram_buf,
    pooled,
    packed,
    part,
    msg_send,
    msg_buf,
    fin,
    load_sem,
    halo_send,
    halo_recv,
    heads_send,
    heads_recv,
    gram_ssem,
    gram_rsem,
    msg_ssem,
    msg_rsem,
    fin_ssem,
    fin_rsem,
):
    n_gx, n_gz, n_ta = sizes
    count = n_gx * n_gz * n_ta
    trainers = n_gx * n_ta
    cx, cz, depth = x_ref.shape
    ex, ez = cx + 2 * HX, cz + 2 * HZ
    elements = owner_ref.shape[0]
    half = packed.shape[1] // 2
    chunks = fin.shape[0]
    gx, gz, ta = lax.axis_index("gx"), lax.axis_index("gz"), lax.axis_index("ta")
    me = (gx * n_gz + gz) * n_ta + ta
    row = gx * n_ta + ta

    def coords(d):
        return (d // (n_gz * n_ta), (d // n_ta) % n_gz, d % n_ta)

    load_rhs = pltpu.make_async_copy(
        rhs_hbm, basis.at[1, pl.ds(HX, cx), pl.ds(HZ, cz), :], load_sem.at[0]
    )
    load_diag = pltpu.make_async_copy(
        diag_hbm, diag.at[pl.ds(HX, cx), pl.ds(HZ, cz), :], load_sem.at[1]
    )
    load_rhs.start()
    load_diag.start()

    barrier = pltpu.get_barrier_semaphore()

    def greet(s, carry):
        pl.semaphore_signal(
            barrier, inc=1, device_id=coords((me + s) % count), device_id_type=MESH
        )
        return carry

    lax.fori_loop(1, count, greet, 0)

    basis[0] = jnp.zeros(basis.shape[1:], F32)
    scaled = coup_ref[...] * (2.0 / SPREAD)
    c_hi = scaled.astype(BF16)
    c_lo = (scaled - c_hi.astype(F32)).astype(BF16)
    c_split[0:depth, 0:depth] = c_hi
    c_split[0:depth, depth : 2 * depth] = c_lo
    c_split[depth : 2 * depth, 0:depth] = c_hi
    c_split[depth : 2 * depth, depth : 2 * depth] = c_lo
    heads[row] = head_ref[0]

    load_rhs.wait()
    load_diag.wait()
    pl.semaphore_wait(barrier, count - 1)

    def span(step, ghost, inner):
        if step == 0:
            return (ghost, inner), (ghost, inner)
        if step == 1:
            return (inner, ghost), (0, ghost)
        return (ghost, ghost), (ghost + inner, ghost)

    halos = []
    for i, (dx, dz) in enumerate(DIRS):
        (sx, nx), (tx, unused_nx) = span(dx, HX, cx)
        (sz, nz), (tz, unused_nz) = span(dz, HZ, cz)
        there = (row + dx + trainers) % trainers
        target = (there // n_ta, (gz + dz + n_gz) % n_gz, there % n_ta)
        for j, ref in enumerate((basis.at[1], diag)):
            halos.append(
                pltpu.make_async_remote_copy(
                    src_ref=ref.at[pl.ds(sx, nx), pl.ds(sz, nz), :],
                    dst_ref=ref.at[pl.ds(tx, nx), pl.ds(tz, nz), :],
                    send_sem=halo_send.at[j, i],
                    recv_sem=halo_recv.at[j, i],
                    device_id=target,
                    device_id_type=MESH,
                )
            )
    for copy in halos:
        copy.start()

    def send_heads(s, carry):
        there = (row + s) % trainers
        pltpu.make_async_remote_copy(
            src_ref=heads.at[row],
            dst_ref=heads.at[row],
            send_sem=heads_send,
            recv_sem=heads_recv,
            device_id=(there // n_ta, gz, there % n_ta),
            device_id_type=MESH,
        ).start()
        return carry

    lax.fori_loop(1, trainers, send_heads, 0)
    for copy in halos:
        copy.wait()

    rows = PLANES * ez

    def grow(k, carry):
        def planes(j, inner_carry):
            x0 = 1 + PLANES * j
            cur = basis[k + 1, pl.ds(x0, PLANES)].reshape(rows, depth)
            up = basis[k + 1, pl.ds(x0 - 1, PLANES)].reshape(rows, depth)
            down = basis[k + 1, pl.ds(x0 + 1, PLANES)].reshape(rows, depth)
            prev = basis[k, pl.ds(x0, PLANES)].reshape(rows, depth)
            own = diag[pl.ds(x0, PLANES)].reshape(rows, depth)
            hi = cur.astype(BF16)
            lo = (cur - hi.astype(F32)).astype(BF16)
            prod = jnp.dot(
                jnp.concatenate([hi, lo], axis=1), c_split[...], preferred_element_type=F32
            )
            beside = (up + down) + (pltpu.roll(cur, 1, 0) + pltpu.roll(cur, rows - 1, 0))
            horizontal = ((own + (4.0 - CENTRE)) * cur - beside) * (2.0 / SPREAD)
            new = horizontal + (prod[:, 0:depth] + prod[:, depth : 2 * depth]) - prev
            basis[k + 2, pl.ds(x0, PLANES)] = new.reshape(PLANES, ez, depth)
            return inner_carry

        return lax.fori_loop(0, (ex - 2) // PLANES, planes, carry)

    lax.fori_loop(0, ITERS, grow, 0)

    pairs = [(i, j) for i in range(ITERS + 1) for j in range(i, ITERS + 1)]
    spot = {pair: k for k, pair in enumerate(pairs)}

    def gram_plane(x, sums):
        sums = list(sums)
        for z in range(0, cz, 8):
            vecs = [basis[k + 1, HX + x, HZ + z : HZ + z + 8, :] for k in range(ITERS + 1)]
            for q, (i, j) in enumerate(pairs):
                sums[q] = sums[q] + vecs[i] * vecs[j]
        return tuple(sums)

    sums = lax.fori_loop(
        0, cx, gram_plane, tuple(jnp.zeros((8, depth), F32) for unused in pairs)
    )
    lane = lax.broadcasted_iota(jnp.int32, (8, depth), 1)
    mine = jnp.zeros((8, depth), F32)
    for q, value in enumerate(sums):
        mine = mine + jnp.where(lane == q, jnp.sum(value, axis=1, keepdims=True), 0.0)
    mine = jnp.sum(mine, axis=0, keepdims=True)
    gram_send[...] = mine
    gram_buf[me] = mine

    def send_gram(s, carry):
        pltpu.make_async_remote_copy(
            src_ref=gram_send,
            dst_ref=gram_buf.at[me],
            send_sem=gram_ssem,
            recv_sem=gram_rsem,
            device_id=coords((me + s) % count),
            device_id_type=MESH,
        ).start()
        return carry

    lax.fori_loop(1, count, send_gram, 0)

    def all_bytes(ref, number, sem):
        there = ref.at[pl.ds(0, number)]
        return pltpu.make_async_copy(there, there, sem)

    owner = owner_ref[...]
    trainer_ids = lax.broadcasted_iota(jnp.int32, (elements, 128), 1)
    hits = jnp.where(owner == trainer_ids, 1.0, 0.0).astype(BF16)
    same = dot_lanes(hits, hits)
    e_row = lax.broadcasted_iota(jnp.int32, (elements, elements), 0)
    e_col = lax.broadcasted_iota(jnp.int32, (elements, elements), 1)
    rank = jnp.sum(jnp.where(e_col < e_row, same, 0.0), axis=1, keepdims=True)
    slot = owner.astype(F32) * (2.0 * half) + rank
    slot_ids = lax.broadcasted_iota(jnp.int32, (elements, trainers * 2 * half), 1).astype(F32)
    place_hidden = jnp.where(slot == slot_ids, 1.0, 0.0).astype(BF16)
    place_back = jnp.where(slot + half == slot_ids, 1.0, 0.0).astype(BF16)
    place = jnp.concatenate([place_hidden, place_back], axis=0)
    neigh = neigh_ref[...]
    links = jnp.zeros((elements, elements), F32)
    for j in range(neigh.shape[1]):
        links = links + jnp.where(neigh[:, j : j + 1] == e_col, 1.0, 0.0)
    links = links.astype(BF16)
    pool_cols = lax.broadcasted_iota(jnp.int32, (elements, elements * EL), 1)
    pool_rows = lax.broadcasted_iota(jnp.int32, (elements, elements * EL), 0) * EL
    pool_map = jnp.where(
        (pool_cols >= pool_rows) & (pool_cols < pool_rows + EL), 1.0, 0.0
    ).astype(F32)

    all_bytes(gram_buf, count - 1, gram_rsem).wait()
    total = jnp.sum(gram_buf[...], axis=0)

    gram = {}
    for (i, j), q in spot.items():
        value = jnp.broadcast_to(total[0:1, q : q + 1], (8, depth))
        gram[i, j] = value
        gram[j, i] = value

    def inner(a, b):
        return tree_sum(
            a[i] * tree_sum(gram[i, j] * b[j] for j in range(len(b))) for i in range(len(a))
        )

    def operate(a):
        out = []
        for i in range(len(a) + 1):
            terms = []
            if i < len(a):
                terms.append(CENTRE * a[i])
            if i >= 1:
                terms.append((SPREAD / 2) * a[i - 1])
            if i + 1 < len(a):
                terms.append((SPREAD / 2) * a[i + 1])
            out.append(tree_sum(terms))
        return out

    one = jnp.ones((8, depth), F32)
    res, way, sol = [one], [one], []
    norm_now = gram[0, 0]
    for it in range(ITERS):
        applied = operate(way)
        step = norm_now / inner(way, applied)
        sol = [
            sol[i] + step * way[i] if i < len(sol) else step * way[i] for i in range(len(way))
        ]
        res = [
            res[i] - step * applied[i] if i < len(res) else -(step * applied[i])
            for i in range(len(applied))
        ]
        if it < ITERS - 1:
            norm_next = inner(res, res)
            ratio = norm_next / norm_now
            way = [res[i] + ratio * way[i] if i < len(way) else res[i] for i in range(len(res))]
            norm_now = norm_next

    def combine(coefs, x0):
        return tree_sum(
            coefs[k][None]
            * basis[k + 1, pl.ds(HX + x0, EL), HZ : HZ + cz, :].reshape(EL * cz // 8, 8, depth)
            for k in range(len(coefs))
        ).reshape(EL, cz, depth)

    def solve_planes(g, carry):
        field = combine(sol, g * EL)
        x_ref[pl.ds(g * EL, EL)] = field
        pooled[pl.ds(pl.multiple_of(g * cz, cz), cz), :] = jnp.sum(field, axis=0)
        return carry

    lax.fori_loop(0, cx // EL, solve_planes, 0)

    feat = (
        jnp.dot(
            pool_map, pooled[...], precision=lax.Precision.HIGHEST, preferred_element_type=F32
        )
        * (1.0 / EL)
    )
    shear = (feat[:, 1:2] - feat[:, 0:1]).astype(BF16).astype(F32)
    wall_feat = feat.astype(BF16)
    graph_mean = (jnp.dot(links, wall_feat, preferred_element_type=F32) * 0.25).astype(BF16)
    node_input = jnp.concatenate([wall_feat, graph_mean], axis=1)
    preact = jnp.dot(node_input, w_in_ref[...], preferred_element_type=F32)
    pre_sig = sigmoid(preact)
    hidden = (preact * pre_sig).astype(BF16)
    all_bytes(heads, trainers - 1, heads_recv).wait()

    def forward(t, acc):
        value = jnp.dot(hidden, heads[t], preferred_element_type=F32)
        return jnp.where(owner == t, value, acc)

    group = 16
    def forward_group(g, acc):
        for t in range(group):
            acc = forward(g * group + t, acc)
        return acc

    head_pre = lax.fori_loop(
        0, trainers // group, forward_group, jnp.zeros((elements, depth), F32)
    )
    head_sig = sigmoid(head_pre)
    head_out = head_pre * head_sig
    w_out = w_out_ref[...]
    predicted = jnp.sum(head_out * w_out, axis=1, keepdims=True)
    misfit = (predicted - shear) * (1.0 / elements)
    out_part = jnp.sum(misfit * head_out, axis=0, keepdims=True)
    head_back_f = misfit * w_out * (head_sig * (1.0 + head_pre * (1.0 - head_sig)))
    head_back = head_back_f.astype(BF16)
    head_back_f = head_back.astype(F32)

    def backward_group(g, acc):
        for i in range(group):
            t = g * group + i
            acc = acc + dot_lanes(
                jnp.where(owner == t, head_back_f, 0.0).astype(BF16), heads[t]
            )
        return acc

    hidden_back = lax.fori_loop(
        0, trainers // group, backward_group, jnp.zeros((elements, depth), F32)
    ).astype(BF16)
    preact_back = (
        hidden_back.astype(F32) * (pre_sig * (1.0 + preact * (1.0 - pre_sig)))
    ).astype(BF16)
    part[...] = dot_rows(node_input, preact_back)
    packed[...] = (
        dot_rows(place, jnp.concatenate([hidden, head_back], axis=0))
        .astype(BF16)
        .reshape(packed.shape)
    )

    out_hi = out_part.astype(BF16).astype(F32)
    out_lo = out_part - out_hi
    sub = lax.broadcasted_iota(jnp.int32, (8, depth), 0)
    out_rows = jnp.where(sub == 0, out_hi, jnp.where(sub == 1, out_lo, 0.0))

    def message(d):
        chunk = part[pl.ds(pl.multiple_of((d % chunks) * 8, 8), 8), :]
        trainer = (d // (n_gz * n_ta)) * n_ta + d % n_ta
        tail = jnp.concatenate([chunk, out_rows], axis=0).astype(BF16)
        return packed[trainer], tail

    def send_message(s, carry):
        d = (me + s) % count
        routed, tail = message(d)
        msg_send[d, 0 : 2 * half, :] = routed
        msg_send[d, 2 * half : 2 * half + 16, :] = tail
        pltpu.make_async_remote_copy(
            src_ref=msg_send.at[d],
            dst_ref=msg_buf.at[me],
            send_sem=msg_ssem,
            recv_sem=msg_rsem,
            device_id=coords(d),
            device_id_type=MESH,
        ).start()
        return carry

    lax.fori_loop(1, count, send_message, 0)
    routed, tail = message(me)
    msg_buf[me, 0 : 2 * half, :] = routed
    msg_buf[me, 2 * half : 2 * half + 16, :] = tail

    def residual_planes(g, carry):
        r_ref[pl.ds(g * EL, EL)] = combine(res, g * EL)
        return carry

    lax.fori_loop(0, cx // EL, residual_planes, 0)

    all_bytes(msg_buf, count - 1, msg_rsem).wait()
    block = 32

    def sum_tails(b, acc):
        start = b * block
        return acc + jnp.sum(
            msg_buf[pl.ds(start, block), 2 * half : 2 * half + 16, :].astype(F32), axis=0
        )

    tails = lax.fori_loop(0, count // block, sum_tails, jnp.zeros((16, depth), F32))

    def send_fin(s, carry):
        pltpu.make_async_remote_copy(
            src_ref=fin.at[me],
            dst_ref=fin.at[me],
            send_sem=fin_ssem,
            recv_sem=fin_rsem,
            device_id=coords((me + s) % count),
            device_id_type=MESH,
        ).start()
        return carry

    if chunks == count:
        fin[me] = tails[0:8]
        lax.fori_loop(1, count, send_fin, 0)
    else:

        @pl.when(me < chunks)
        def own_chunk():
            fin[me] = tails[0:8]
            lax.fori_loop(1, count, send_fin, 0)

    og_ref[...] = tails[8:9] + tails[9:10]

    def sum_heads(b, acc):
        both = msg_buf[pl.ds(b * block, block), 0 : 2 * half, :].astype(F32)
        hid = both[:, 0:half].reshape(block * half, depth).astype(BF16)
        back = both[:, half : 2 * half].reshape(block * half, depth).astype(BF16)
        return acc + dot_rows(hid, back)

    hg_ref[0] = lax.fori_loop(0, count // block, sum_heads, jnp.zeros((depth, depth), F32))

    if chunks == count:
        all_bytes(fin, count - 1, fin_rsem).wait()
        all_bytes(fin, count - 1, fin_ssem).wait()
    else:

        @pl.when(me < chunks)
        def owner_waits():
            all_bytes(fin, chunks - 1, fin_rsem).wait()

            def one_send(s, carry):
                pltpu.make_async_copy(fin.at[me], fin.at[me], fin_ssem).wait()
                return carry

            lax.fori_loop(1, count, one_send, 0)

        @pl.when(me >= chunks)
        def others_wait():
            all_bytes(fin, chunks, fin_rsem).wait()

    ig_ref[...] = fin[...].reshape(ig_ref.shape)
    all_bytes(heads, trainers - 1, heads_send).wait()
    all_bytes(gram_buf, count - 1, gram_ssem).wait()
    all_bytes(msg_buf, count - 1, msg_ssem).wait()


def local(
    sizes,
    right_side,
    diagonal,
    coupling,
    wall_owner,
    neighbours,
    input_weight,
    head_weights,
    output_weight,
):
    n_gx, n_gz, n_ta = sizes
    count, trainers = n_gx * n_gz * n_ta, n_gx * n_ta
    cx, cz, depth = right_side.shape
    ex, ez = cx + 2 * HX, cz + 2 * HZ
    elements = wall_owner.shape[0]
    capacity = max(2, 2 * elements // trainers)
    half = -(-capacity // 8) * 8
    wide = input_weight.shape[0]
    chunks = min(count, wide // 8)
    vmem = pl.BlockSpec(memory_space=pltpu.VMEM)
    hbm = pl.BlockSpec(memory_space=pl.ANY)
    dma = pltpu.SemaphoreType.DMA
    field, residual, input_grad, head_grad, output_grad = pl.pallas_call(
        functools.partial(kernel, sizes),
        out_shape=(
            jax.ShapeDtypeStruct(right_side.shape, F32),
            jax.ShapeDtypeStruct(right_side.shape, F32),
            jax.ShapeDtypeStruct((wide, depth), F32),
            jax.ShapeDtypeStruct((1, depth, depth), F32),
            jax.ShapeDtypeStruct((1, depth), F32),
        ),
        in_specs=[hbm, hbm] + [vmem] * 6,
        out_specs=(vmem,) * 5,
        scratch_shapes=[
            pltpu.VMEM((ITERS + 2, ex, ez, depth), F32),
            pltpu.VMEM((ex, ez, depth), F32),
            pltpu.VMEM((trainers, depth, depth), BF16),
            pltpu.VMEM((2 * depth, 2 * depth), BF16),
            pltpu.VMEM((1, depth), F32),
            pltpu.VMEM((count, 1, depth), F32),
            pltpu.VMEM((elements * EL, depth), F32),
            pltpu.VMEM((trainers, 2 * half, depth), BF16),
            pltpu.VMEM((wide, depth), F32),
            pltpu.VMEM((count, 2 * half + 16, depth), BF16),
            pltpu.VMEM((count, 2 * half + 16, depth), BF16),
            pltpu.VMEM((chunks, 8, depth), F32),
            dma((2,)),
            dma((2, len(DIRS))),
            dma((2, len(DIRS))),
            dma,
            dma,
            dma,
            dma,
            dma,
            dma,
            dma,
            dma,
        ],
        compiler_params=pltpu.CompilerParams(
            collective_id=0, has_side_effects=True, vmem_limit_bytes=44 * 1024 * 1024
        ),
    )(
        right_side,
        diagonal,
        coupling,
        wall_owner,
        neighbours,
        input_weight,
        head_weights,
        output_weight.reshape(1, -1),
    )
    return (field, residual, input_grad, head_grad, output_grad.reshape(-1))


def solution(mesh):
    placed = (
        P(("gx", "ta"), "gz", None),
        P(("gx", "ta"), "gz", None),
        P(),
        P(("gx", "gz", "ta"), None),
        P(("gx", "gz", "ta"), None),
        P(),
        P(("gx", "ta"), None, None),
        P(),
    )
    sizes = tuple(mesh.shape[name] for name in ("gx", "gz", "ta"))
    return jax.shard_map(
        functools.partial(local, sizes),
        mesh=mesh,
        in_specs=placed,
        out_specs=(
            P(("gx", "ta"), "gz", None),
            P(("gx", "ta"), "gz", None),
            P(),
            P(("gx", "ta"), None, None),
            P(),
        ),
        check_vma=False,
    )
```

```python
import functools
import jax
import jax.numpy as jnp
from jax import lax
from jax.experimental import pallas as pl
from jax.experimental.pallas import tpu as pltpu
from jax.sharding import PartitionSpec as P

EL = 4
ITERS = 6
HX = ITERS
HZ = 8
CENTRE = 5.3
SPREAD = 5.4
PLANES = 14
MESH = pl.DeviceIdType.MESH
F32 = jnp.float32
BF16 = jnp.bfloat16

def tree_sum(terms):
    terms = list(terms)
    while len(terms) > 1:
        terms = [
            terms[i] + terms[i + 1] if i + 1 < len(terms) else terms[i]
            for i in range(0, len(terms), 2)
        ]
    return terms[0]


def sigmoid(v):
    return 1.0 / (1.0 + jnp.exp(-v))


def dot_rows(a, b):
    return lax.dot_general(a, b, (((0,), (0,)), ((), ())), preferred_element_type=F32)


def dot_lanes(a, b):
    return lax.dot_general(a, b, (((1,), (1,)), ((), ())), preferred_element_type=F32)


def kernel(
    sizes,
    rhs_hbm,
    diag_hbm,
    coup_hbm,
    owner_hbm,
    neigh_hbm,
    w_in_hbm,
    head_hbm,
    w_out_hbm,
    x_ref,
    r_ref,
    ig_ref,
    hg_ref,
    og_ref,
    basis,
    diag,
    coup_ref,
    owner_ref,
    neigh_ref,
    w_in_ref,
    head_ref,
    w_out_ref,
    c_split,
    gram_pair,
    gram_buf,
    pooled,
    fwd_send,
    fwd_buf,
    ret_send,
    ret_buf,
    part_send,
    part_buf,
    pair_heads,
    pair_sums,
    fin,
    load_sem,
    halo_send,
    halo_recv,
    corner_send,
    corner_recv,
    group_send,
    group_recv,
):
    n_gx, n_gz, n_ta = sizes
    trainers = n_gx * n_ta
    cx, cz, depth = x_ref.shape
    ex, ez = cx + 2 * HX, cz + 2 * HZ
    elements = owner_ref.shape[1]
    half = fwd_buf.shape[1] // 2
    chunks, chunk = fin.shape[0], fin.shape[1]
    gx, gz, ta = lax.axis_index("gx"), lax.axis_index("gz"), lax.axis_index("ta")
    row = gx * n_ta + ta

    def in_row(there):
        return (there // n_ta, gz, there % n_ta)

    loads = [
        pltpu.make_async_copy(source, target, load_sem.at[i])
        for i, (source, target) in enumerate(
            (
                (rhs_hbm, basis.at[1, pl.ds(HX, cx), pl.ds(HZ, cz), :]),
                (diag_hbm, diag.at[pl.ds(HX, cx), pl.ds(HZ, cz), :]),
                (coup_hbm, coup_ref),
                (owner_hbm, owner_ref),
                (neigh_hbm, neigh_ref),
                (w_in_hbm, w_in_ref),
                (head_hbm, head_ref),
                (w_out_hbm, w_out_ref),
            )
        )
    ]
    for load in loads:
        load.start()

    barrier = pltpu.get_barrier_semaphore()

    def greet(s, carry):
        pl.semaphore_signal(
            barrier, inc=1, device_id=in_row((row + s) % trainers), device_id_type=MESH
        )
        return carry

    lax.fori_loop(1, trainers, greet, 0)
    for s in range(1, n_gz):
        pl.semaphore_signal(
            barrier, inc=1, device_id=(gx, (gz + s) % n_gz, ta), device_id_type=MESH
        )

    basis[0] = jnp.zeros(basis.shape[1:], F32)
    for load in loads:
        load.wait()
    scaled = coup_ref[...] * (2.0 / SPREAD)
    c_hi = scaled.astype(BF16)
    c_lo = (scaled - c_hi.astype(F32)).astype(BF16)
    c_split[0:depth, 0:depth] = c_hi
    c_split[0:depth, depth : 2 * depth] = c_lo
    c_split[depth : 2 * depth, 0:depth] = c_hi
    c_split[depth : 2 * depth, depth : 2 * depth] = c_lo
    pl.semaphore_wait(barrier, trainers - 1 + n_gz - 1)

    def edge_copy(ref, src_x, dst_x, nx, src_z, dst_z, nz, target, sends, recvs, i):
        return pltpu.make_async_remote_copy(
            src_ref=ref.at[pl.ds(src_x, nx), pl.ds(src_z, nz), :],
            dst_ref=ref.at[pl.ds(dst_x, nx), pl.ds(dst_z, nz), :],
            send_sem=sends.at[i],
            recv_sem=recvs.at[i],
            device_id=target,
            device_id_type=MESH,
        )

    fields = (basis.at[1], diag)
    after, before = in_row((row + 1) % trainers), in_row((row + trainers - 1) % trainers)
    higher, lower = (gx, (gz + 1) % n_gz, ta), (gx, (gz + n_gz - 1) % n_gz, ta)
    x_copies, z_copies, corners = [], [], []
    for j, ref in enumerate(fields):
        wide = HX - j
        for up, (target, src, dst) in enumerate(
            ((after, HX + cx - wide, HX - wide), (before, HX, HX + cx))
        ):
            x_copies.append(
                edge_copy(
                    ref, src, dst, wide, HZ, HZ, cz, target, halo_send, halo_recv, 2 * j + up
                )
            )
    for j, ref in enumerate(fields):
        for up, (target, src, dst) in enumerate(((higher, cz, 0), (lower, HZ, HZ + cz))):
            z_copies.append(
                edge_copy(
                    ref, HX, HX, cx, src, dst, HZ, target, halo_send, halo_recv, 4 + 2 * j + up
                )
            )
            for side, x0 in enumerate((1, HX + cx)):
                corners.append(
                    edge_copy(
                        ref, x0, x0, HX - 1, src, dst, HZ, target,
                        corner_send, corner_recv, 4 * j + 2 * up + side,
                    )
                )
    for copy in x_copies + z_copies:
        copy.start()

    owner = owner_ref[...]
    ids = lax.broadcasted_iota(jnp.int32, (128, elements), 0)
    hits = jnp.where(owner == ids, 1.0, 0.0).astype(BF16)
    same = dot_rows(hits, hits)
    e_row = lax.broadcasted_iota(jnp.int32, (elements, elements), 0)
    e_col = lax.broadcasted_iota(jnp.int32, (elements, elements), 1)
    rank = jnp.sum(jnp.where(e_row < e_col, same, 0.0), axis=0, keepdims=True)
    slot = owner.astype(F32) * (2.0 * half) + rank
    slot_ids = lax.broadcasted_iota(jnp.int32, (trainers * 2 * half, elements), 0).astype(F32)
    place_hidden = jnp.where(slot == slot_ids, 1.0, 0.0).astype(BF16)
    place_shear = jnp.where(slot + half == slot_ids, 1.0, 0.0).astype(BF16)
    place = jnp.concatenate([place_hidden, place_shear], axis=1)
    neigh = neigh_ref[...]
    links = jnp.zeros((elements, elements), F32)
    for j in range(neigh.shape[0]):
        links = links + jnp.where(neigh[j : j + 1, :] == e_row, 1.0, 0.0)
    links = links.astype(BF16)
    pool_cols = lax.broadcasted_iota(jnp.int32, (elements, elements * EL), 1)
    pool_rows = lax.broadcasted_iota(jnp.int32, (elements, elements * EL), 0) * EL
    pool_map = jnp.where(
        (pool_cols >= pool_rows) & (pool_cols < pool_rows + EL), 1.0, 0.0
    ).astype(F32)

    for copy in x_copies:
        copy.wait_recv()
    for copy in corners:
        copy.start()
    for copy in z_copies + corners:
        copy.wait_recv()

    rows = PLANES * ez

    def grow(k, carry):
        def planes(j, inner_carry):
            x0 = 1 + PLANES * j
            cur = basis[k + 1, pl.ds(x0, PLANES)].reshape(rows, depth)
            up = basis[k + 1, pl.ds(x0 - 1, PLANES)].reshape(rows, depth)
            down = basis[k + 1, pl.ds(x0 + 1, PLANES)].reshape(rows, depth)
            prev = basis[k, pl.ds(x0, PLANES)].reshape(rows, depth)
            own = diag[pl.ds(x0, PLANES)].reshape(rows, depth)
            hi = cur.astype(BF16)
            lo = (cur - hi.astype(F32)).astype(BF16)
            prod = jnp.dot(
                jnp.concatenate([hi, lo], axis=1), c_split[...], preferred_element_type=F32
            )
            beside = (up + down) + (pltpu.roll(cur, 1, 0) + pltpu.roll(cur, rows - 1, 0))
            horizontal = ((own + (4.0 - CENTRE)) * cur - beside) * (2.0 / SPREAD)
            new = horizontal + (prod[:, 0:depth] + prod[:, depth : 2 * depth]) - prev
            basis[k + 2, pl.ds(x0, PLANES)] = new.reshape(PLANES, ez, depth)
            return inner_carry

        return lax.fori_loop(0, (ex - 2) // PLANES, planes, carry)

    lax.fori_loop(0, ITERS, grow, 0)

    pairs = [(i, j) for i in range(ITERS + 1) for j in range(i, ITERS + 1)]
    spot = {pair: k for k, pair in enumerate(pairs)}

    def gram_plane(x, sums):
        sums = list(sums)
        for z in range(0, cz, 8):
            vecs = [basis[k + 1, HX + x, HZ + z : HZ + z + 8, :] for k in range(ITERS + 1)]
            for q, (i, j) in enumerate(pairs):
                sums[q] = sums[q] + vecs[i] * vecs[j]
        return tuple(sums)

    sums = lax.fori_loop(
        0, cx, gram_plane, tuple(jnp.zeros((8, depth), F32) for unused in pairs)
    )
    lane = lax.broadcasted_iota(jnp.int32, (8, depth), 1)
    mine = jnp.zeros((8, depth), F32)
    for q, value in enumerate(sums):
        mine = mine + jnp.where(lane == q, jnp.sum(value, axis=1, keepdims=True), 0.0)
    mine = jnp.sum(mine, axis=0, keepdims=True)

    def all_bytes(ref, number, sem):
        there = ref.at[pl.ds(0, number)]
        return pltpu.make_async_copy(there, there, sem)

    def to_pair(ref, i):
        for s in range(1, n_gz):
            pltpu.make_async_remote_copy(
                src_ref=ref.at[gz],
                dst_ref=ref.at[gz],
                send_sem=group_send.at[i],
                recv_sem=group_recv.at[i],
                device_id=(gx, (gz + s) % n_gz, ta),
                device_id_type=MESH,
            ).start()

    def to_row(source, ref, i):
        def send(s, carry):
            there = (row + s) % trainers
            pltpu.make_async_remote_copy(
                src_ref=source(there),
                dst_ref=ref.at[row],
                send_sem=group_send.at[i],
                recv_sem=group_recv.at[i],
                device_id=in_row(there),
                device_id_type=MESH,
            ).start()
            return carry

        lax.fori_loop(1, trainers, send, 0)

    gram_pair[gz] = mine
    to_pair(gram_pair, 0)
    all_bytes(gram_pair, n_gz - 1, group_recv.at[0]).wait()
    gram_buf[row] = jnp.sum(gram_pair[...], axis=0)
    to_row(lambda there: gram_buf.at[row], gram_buf, 1)
    all_bytes(gram_buf, trainers - 1, group_recv.at[1]).wait()
    total = jnp.sum(gram_buf[...], axis=0)

    gram = {}
    for (i, j), q in spot.items():
        value = jnp.broadcast_to(total[0:1, q : q + 1], (8, depth))
        gram[i, j] = value
        gram[j, i] = value

    def inner(a, b):
        return tree_sum(
            a[i] * tree_sum(gram[i, j] * b[j] for j in range(len(b))) for i in range(len(a))
        )

    def operate(a):
        out = []
        for i in range(len(a) + 1):
            terms = []
            if i < len(a):
                terms.append(CENTRE * a[i])
            if i >= 1:
                terms.append((SPREAD / 2) * a[i - 1])
            if i + 1 < len(a):
                terms.append((SPREAD / 2) * a[i + 1])
            out.append(tree_sum(terms))
        return out

    one = jnp.ones((8, depth), F32)
    res, way, sol = [one], [one], []
    norm_now = gram[0, 0]
    for it in range(ITERS):
        applied = operate(way)
        step = norm_now / inner(way, applied)
        sol = [
            sol[i] + step * way[i] if i < len(sol) else step * way[i] for i in range(len(way))
        ]
        res = [
            res[i] - step * applied[i] if i < len(res) else -(step * applied[i])
            for i in range(len(applied))
        ]
        if it < ITERS - 1:
            norm_next = inner(res, res)
            ratio = norm_next / norm_now
            way = [res[i] + ratio * way[i] if i < len(way) else res[i] for i in range(len(res))]
            norm_now = norm_next

    def combine(coefs, x0):
        return tree_sum(
            coefs[k][None]
            * basis[k + 1, pl.ds(HX + x0, EL), HZ : HZ + cz, :].reshape(EL * cz // 8, 8, depth)
            for k in range(len(coefs))
        ).reshape(EL, cz, depth)

    def solve_planes(g, carry):
        field = combine(sol, g * EL)
        x_ref[pl.ds(g * EL, EL)] = field
        pooled[pl.ds(pl.multiple_of(g * cz, cz), cz), :] = jnp.sum(field, axis=0)
        return carry

    lax.fori_loop(0, cx // EL, solve_planes, 0)

    feat = (
        jnp.dot(
            pool_map, pooled[...], precision=lax.Precision.HIGHEST, preferred_element_type=F32
        )
        * (1.0 / EL)
    )
    shear = (feat[:, 1:2] - feat[:, 0:1]).astype(BF16)
    wall_feat = feat.astype(BF16)
    graph_mean = (dot_rows(links, wall_feat) * 0.25).astype(BF16)
    node_input = jnp.concatenate([wall_feat, graph_mean], axis=1)
    preact = jnp.dot(node_input, w_in_ref[...], preferred_element_type=F32)
    pre_sig = sigmoid(preact)
    hidden = (preact * pre_sig).astype(BF16)
    shears = jnp.broadcast_to(shear.astype(F32), (elements, depth)).astype(BF16)
    fwd_send[...] = (
        jnp.dot(
            place, jnp.concatenate([hidden, shears], axis=0), preferred_element_type=F32
        )
        .astype(BF16)
        .reshape(fwd_send.shape)
    )
    to_row(lambda there: fwd_send.at[there], fwd_buf, 2)
    fwd_buf[row] = fwd_send[row]

    def residual_planes(g, carry):
        r_ref[pl.ds(g * EL, EL)] = combine(res, g * EL)
        return carry

    lax.fori_loop(0, cx // EL, residual_planes, 0)

    all_bytes(fwd_buf, trainers - 1, group_recv.at[2]).wait()
    arrived = fwd_buf[...].astype(F32)
    slots = trainers * half
    hid = arrived[:, 0:half].reshape(slots, depth).astype(BF16)
    own_shear = arrived[:, half : 2 * half].reshape(slots, depth)[:, 0:1]
    own_head = head_ref[0]
    head_pre = jnp.dot(hid, own_head, preferred_element_type=F32)
    head_sig = sigmoid(head_pre)
    head_out = head_pre * head_sig
    w_out = w_out_ref[...]
    predicted = jnp.sum(head_out * w_out, axis=1, keepdims=True)
    misfit = (predicted - own_shear) * (1.0 / elements)
    out_part = jnp.sum(misfit * head_out, axis=0, keepdims=True)
    head_back = (
        misfit * w_out * (head_sig * (1.0 + head_pre * (1.0 - head_sig)))
    ).astype(BF16)
    back = dot_lanes(head_back, own_head).reshape(trainers, half, depth)
    out_hi = out_part.astype(BF16).astype(F32)
    out_lo = out_part - out_hi
    sub = lax.broadcasted_iota(jnp.int32, (half, depth), 0)
    out_rows = jnp.where(sub == 0, out_hi, jnp.where(sub == 1, out_lo, 0.0))
    ret_send[...] = jnp.concatenate(
        [back, jnp.broadcast_to(out_rows[None], (trainers, half, depth))], axis=1
    ).astype(BF16)
    to_row(lambda there: ret_send.at[there], ret_buf, 3)
    ret_buf[row] = ret_send[row]
    pair_heads[gz] = dot_rows(hid, head_back)
    to_pair(pair_heads, 4)
    slope = pre_sig * (1.0 + preact * (1.0 - pre_sig))

    all_bytes(ret_buf, trainers - 1, group_recv.at[3]).wait()
    returned = ret_buf[...]
    hidden_back = dot_rows(place_hidden, returned.reshape(trainers * 2 * half, depth))
    preact_back = (hidden_back * slope).astype(BF16)
    part = dot_rows(node_input, preact_back).astype(BF16)
    part_send[...] = part.reshape(part_send.shape)
    to_row(lambda there: part_send.at[there % chunks], part_buf, 5)
    part_buf[row] = part_send[row % chunks]
    out_plane = jnp.sum(returned[:, half : 2 * half].astype(F32), axis=0)

    all_bytes(part_buf, trainers - 1, group_recv.at[5]).wait()
    pair_sums[gz] = jnp.concatenate(
        [jnp.sum(part_buf[...].astype(F32), axis=0), out_plane], axis=0
    )
    to_pair(pair_sums, 6)
    all_bytes(pair_sums, n_gz - 1, group_recv.at[6]).wait()
    sums = jnp.sum(pair_sums[...], axis=0)

    if chunks == trainers:
        fin[row] = sums[0:chunk].astype(BF16)
        to_row(lambda there: fin.at[row], fin, 7)
    else:

        @pl.when(row < chunks)
        def own_chunk():
            fin[row] = sums[0:chunk].astype(BF16)
            to_row(lambda there: fin.at[row], fin, 7)

    og_ref[...] = sums[chunk : chunk + 1] + sums[chunk + 1 : chunk + 2]
    all_bytes(pair_heads, n_gz - 1, group_recv.at[4]).wait()
    hg_ref[0] = jnp.sum(pair_heads[...], axis=0)

    for copy in x_copies + z_copies + corners:
        copy.wait_send()
    for ref, number, i in (
        (gram_pair, n_gz, 0),
        (gram_buf, trainers, 1),
        (fwd_buf, trainers, 2),
        (ret_buf, trainers, 3),
        (pair_heads, n_gz, 4),
        (part_buf, trainers, 5),
        (pair_sums, n_gz, 6),
    ):
        all_bytes(ref, number - 1, group_send.at[i]).wait()

    if chunks == trainers:
        all_bytes(fin, trainers - 1, group_recv.at[7]).wait()
        all_bytes(fin, trainers - 1, group_send.at[7]).wait()
    else:

        @pl.when(row < chunks)
        def owner_waits():
            all_bytes(fin, chunks - 1, group_recv.at[7]).wait()

            def one_send(s, carry):
                pltpu.make_async_copy(fin.at[row], fin.at[row], group_send.at[7]).wait()
                return carry

            lax.fori_loop(1, trainers, one_send, 0)

        @pl.when(row >= chunks)
        def others_wait():
            all_bytes(fin, chunks, group_recv.at[7]).wait()

    ig_ref[...] = fin[...].astype(F32).reshape(ig_ref.shape)


def hand_over(*refs):
    count = len(refs) // 2
    sems = refs[-1]
    copies = [
        pltpu.make_async_copy(refs[i], refs[count + i], sems.at[i]) for i in range(count)
    ]
    for copy in copies:
        copy.start()
    for copy in copies:
        copy.wait()


def local(
    sizes,
    right_side,
    diagonal,
    coupling,
    wall_owner,
    neighbours,
    input_weight,
    head_weights,
    output_weight,
):
    n_gx, n_gz, n_ta = sizes
    trainers = n_gx * n_ta
    cx, cz, depth = right_side.shape
    ex, ez = cx + 2 * HX, cz + 2 * HZ
    elements = wall_owner.shape[0]
    capacity = max(2, 2 * elements // trainers)
    half = -(-capacity // 8) * 8
    wide = input_weight.shape[0]
    chunks = min(trainers, wide // 16)
    chunk = wide // chunks
    vmem = pl.BlockSpec(memory_space=pltpu.VMEM)
    hbm = pl.BlockSpec(memory_space=pl.ANY)
    dma = pltpu.SemaphoreType.DMA
    rows = (trainers, 2 * half, depth)
    shapes = (
        jax.ShapeDtypeStruct(right_side.shape, F32),
        jax.ShapeDtypeStruct(right_side.shape, F32),
        jax.ShapeDtypeStruct((wide, depth), F32),
        jax.ShapeDtypeStruct((1, depth, depth), F32),
        jax.ShapeDtypeStruct((1, depth), F32),
    )
    results = pl.pallas_call(
        functools.partial(kernel, sizes),
        out_shape=shapes,
        in_specs=[hbm] * 8,
        out_specs=(vmem,) * 5,
        scratch_shapes=[
            pltpu.VMEM((ITERS + 2, ex, ez, depth), F32),
            pltpu.VMEM((ex, ez, depth), F32),
            pltpu.VMEM((depth, depth), F32),
            pltpu.VMEM((1, elements), jnp.int32),
            pltpu.VMEM((neighbours.shape[1], elements), jnp.int32),
            pltpu.VMEM((wide, depth), BF16),
            pltpu.VMEM((1, depth, depth), BF16),
            pltpu.VMEM((1, depth), F32),
            pltpu.VMEM((2 * depth, 2 * depth), BF16),
            pltpu.VMEM((n_gz, 1, depth), F32),
            pltpu.VMEM((trainers, 1, depth), F32),
            pltpu.VMEM((elements * EL, depth), F32),
            pltpu.VMEM(rows, BF16),
            pltpu.VMEM(rows, BF16),
            pltpu.VMEM(rows, BF16),
            pltpu.VMEM(rows, BF16),
            pltpu.VMEM((chunks, chunk, depth), BF16),
            pltpu.VMEM((trainers, chunk, depth), BF16),
            pltpu.VMEM((n_gz, depth, depth), F32),
            pltpu.VMEM((n_gz, chunk + half, depth), F32),
            pltpu.VMEM((chunks, chunk, depth), BF16),
            dma((8,)),
            dma((8,)),
            dma((8,)),
            dma((8,)),
            dma((8,)),
            dma((8,)),
            dma((8,)),
        ],
        compiler_params=pltpu.CompilerParams(
            collective_id=0, has_side_effects=True, vmem_limit_bytes=56 * 1024 * 1024
        ),
    )(
        right_side,
        diagonal,
        coupling,
        wall_owner.reshape(1, -1),
        neighbours.T,
        input_weight,
        head_weights,
        output_weight.reshape(1, -1),
    )
    field, residual, input_grad, head_grad, output_grad = pl.pallas_call(
        hand_over,
        out_shape=shapes,
        in_specs=[hbm] * 5,
        out_specs=(hbm,) * 5,
        scratch_shapes=[dma((5,))],
    )(*results)
    return (field, residual, input_grad, head_grad, output_grad.reshape(-1))


def solution(mesh):
    placed = (
        P(("gx", "ta"), "gz", None),
        P(("gx", "ta"), "gz", None),
        P(),
        P(("gx", "gz", "ta"), None),
        P(("gx", "gz", "ta"), None),
        P(),
        P(("gx", "ta"), None, None),
        P(),
    )
    sizes = tuple(mesh.shape[name] for name in ("gx", "gz", "ta"))
    return jax.shard_map(
        functools.partial(local, sizes),
        mesh=mesh,
        in_specs=placed,
        out_specs=(
            P(("gx", "ta"), "gz", None),
            P(("gx", "ta"), "gz", None),
            P(),
            P(("gx", "ta"), None, None),
            P(),
        ),
        check_vma=False,
    )
```

```python
import functools
import jax
import jax.numpy as jnp
from jax import lax
from jax.experimental import pallas as pl
from jax.experimental.pallas import tpu as pltpu
from jax.sharding import PartitionSpec as P

EL = 4
ITERS = 6
HX = ITERS
HZ = 8
CENTRE = 5.3
SPREAD = 5.4
PLANES = 14
MESH = pl.DeviceIdType.MESH
F32 = jnp.float32
BF16 = jnp.bfloat16

def tree_sum(terms):
    terms = list(terms)
    while len(terms) > 1:
        terms = [
            terms[i] + terms[i + 1] if i + 1 < len(terms) else terms[i]
            for i in range(0, len(terms), 2)
        ]
    return terms[0]


def sigmoid(v):
    return 1.0 / (1.0 + jnp.exp(-v))


def dot_rows(a, b):
    return lax.dot_general(a, b, (((0,), (0,)), ((), ())), preferred_element_type=F32)


def dot_lanes(a, b):
    return lax.dot_general(a, b, (((1,), (1,)), ((), ())), preferred_element_type=F32)


def kernel(
    sizes,
    rhs_hbm,
    diag_hbm,
    coup_hbm,
    owner_hbm,
    neigh_hbm,
    w_in_hbm,
    head_hbm,
    w_out_hbm,
    x_ref,
    r_ref,
    ig_ref,
    hg_ref,
    og_ref,
    basis,
    diag,
    coup_ref,
    owner_ref,
    neigh_ref,
    w_in_ref,
    head_ref,
    w_out_ref,
    c_split,
    gram_pair,
    gram_buf,
    pooled,
    fwd_send,
    fwd_buf,
    ret_send,
    ret_buf,
    part_send,
    part_buf,
    pair_heads,
    pair_sums,
    fin,
    load_sem,
    halo_send,
    halo_recv,
    corner_send,
    corner_recv,
    group_send,
    group_recv,
):
    n_gx, n_gz, n_ta = sizes
    trainers = n_gx * n_ta
    cx, cz, depth = x_ref.shape
    ex, ez = cx + 2 * HX, cz + 2 * HZ
    elements = owner_ref.shape[1]
    half = fwd_buf.shape[1] // 2
    chunks, chunk = fin.shape[0], fin.shape[1]
    gx, gz, ta = lax.axis_index("gx"), lax.axis_index("gz"), lax.axis_index("ta")
    row = gx * n_ta + ta

    def in_row(there):
        return (there // n_ta, gz, there % n_ta)

    loads = [
        pltpu.make_async_copy(source, target, load_sem.at[i])
        for i, (source, target) in enumerate(
            (
                (rhs_hbm, basis.at[1, pl.ds(HX, cx), pl.ds(HZ, cz), :]),
                (diag_hbm, diag.at[pl.ds(HX, cx), pl.ds(HZ, cz), :]),
                (coup_hbm, coup_ref),
                (owner_hbm, owner_ref),
                (neigh_hbm, neigh_ref),
                (w_in_hbm, w_in_ref),
                (head_hbm, head_ref),
                (w_out_hbm, w_out_ref),
            )
        )
    ]
    for load in loads:
        load.start()

    barrier = pltpu.get_barrier_semaphore()

    def greet(s, carry):
        pl.semaphore_signal(
            barrier, inc=1, device_id=in_row((row + s) % trainers), device_id_type=MESH
        )
        return carry

    lax.fori_loop(1, trainers, greet, 0)
    for s in range(1, n_gz):
        pl.semaphore_signal(
            barrier, inc=1, device_id=(gx, (gz + s) % n_gz, ta), device_id_type=MESH
        )

    basis[0] = jnp.zeros(basis.shape[1:], F32)
    for load in loads:
        load.wait()
    scaled = coup_ref[...] * (2.0 / SPREAD)
    c_hi = scaled.astype(BF16)
    c_lo = (scaled - c_hi.astype(F32)).astype(BF16)
    c_split[0:depth, 0:depth] = c_hi
    c_split[0:depth, depth : 2 * depth] = c_lo
    c_split[depth : 2 * depth, 0:depth] = c_hi
    c_split[depth : 2 * depth, depth : 2 * depth] = c_lo
    pl.semaphore_wait(barrier, trainers - 1 + n_gz - 1)

    def edge_copy(ref, src_x, dst_x, nx, src_z, dst_z, nz, target, sends, recvs, i):
        return pltpu.make_async_remote_copy(
            src_ref=ref.at[pl.ds(src_x, nx), pl.ds(src_z, nz), :],
            dst_ref=ref.at[pl.ds(dst_x, nx), pl.ds(dst_z, nz), :],
            send_sem=sends.at[i],
            recv_sem=recvs.at[i],
            device_id=target,
            device_id_type=MESH,
        )

    fields = (basis.at[1], diag)
    after, before = in_row((row + 1) % trainers), in_row((row + trainers - 1) % trainers)
    higher, lower = (gx, (gz + 1) % n_gz, ta), (gx, (gz + n_gz - 1) % n_gz, ta)
    x_copies, z_copies, corners = [], [], []
    for j, ref in enumerate(fields):
        wide = HX - j
        for up, (target, src, dst) in enumerate(
            ((after, HX + cx - wide, HX - wide), (before, HX, HX + cx))
        ):
            x_copies.append(
                edge_copy(
                    ref, src, dst, wide, HZ, HZ, cz, target, halo_send, halo_recv, 2 * j + up
                )
            )
    for j, ref in enumerate(fields):
        for up, (target, src, dst) in enumerate(((higher, cz, 0), (lower, HZ, HZ + cz))):
            z_copies.append(
                edge_copy(
                    ref, HX, HX, cx, src, dst, HZ, target, halo_send, halo_recv, 4 + 2 * j + up
                )
            )
            for side, x0 in enumerate((1, HX + cx)):
                corners.append(
                    edge_copy(
                        ref, x0, x0, HX - 1, src, dst, HZ, target,
                        corner_send, corner_recv, 4 * j + 2 * up + side,
                    )
                )
    for copy in x_copies + z_copies:
        copy.start()

    owner = owner_ref[...]
    ids = lax.broadcasted_iota(jnp.int32, (128, elements), 0)
    hits = jnp.where(owner == ids, 1.0, 0.0).astype(BF16)
    same = dot_rows(hits, hits)
    e_row = lax.broadcasted_iota(jnp.int32, (elements, elements), 0)
    e_col = lax.broadcasted_iota(jnp.int32, (elements, elements), 1)
    rank = jnp.sum(jnp.where(e_row < e_col, same, 0.0), axis=0, keepdims=True)
    slot = owner.astype(F32) * (2.0 * half) + rank
    slot_ids = lax.broadcasted_iota(jnp.int32, (trainers * 2 * half, elements), 0).astype(F32)
    place_hidden = jnp.where(slot == slot_ids, 1.0, 0.0).astype(BF16)
    place_shear = jnp.where(slot + half == slot_ids, 1.0, 0.0).astype(BF16)
    place = jnp.concatenate([place_hidden, place_shear], axis=1)
    neigh = neigh_ref[...]
    links = jnp.zeros((elements, elements), F32)
    for j in range(neigh.shape[0]):
        links = links + jnp.where(neigh[j : j + 1, :] == e_row, 1.0, 0.0)
    links = links.astype(BF16)
    pool_cols = lax.broadcasted_iota(jnp.int32, (elements, elements * EL), 1)
    pool_rows = lax.broadcasted_iota(jnp.int32, (elements, elements * EL), 0) * EL
    pool_map = jnp.where(
        (pool_cols >= pool_rows) & (pool_cols < pool_rows + EL), 1.0, 0.0
    ).astype(F32)

    for copy in x_copies:
        copy.wait_recv()
    for copy in corners:
        copy.start()
    for copy in z_copies + corners:
        copy.wait_recv()

    rows = PLANES * ez

    def grow(k, carry):
        def planes(j, inner_carry):
            x0 = 1 + PLANES * j
            cur = basis[k + 1, pl.ds(x0, PLANES)].reshape(rows, depth)
            up = basis[k + 1, pl.ds(x0 - 1, PLANES)].reshape(rows, depth)
            down = basis[k + 1, pl.ds(x0 + 1, PLANES)].reshape(rows, depth)
            prev = basis[k, pl.ds(x0, PLANES)].reshape(rows, depth)
            own = diag[pl.ds(x0, PLANES)].reshape(rows, depth)
            hi = cur.astype(BF16)
            lo = (cur - hi.astype(F32)).astype(BF16)
            prod = jnp.dot(
                jnp.concatenate([hi, lo], axis=1), c_split[...], preferred_element_type=F32
            )
            beside = (up + down) + (pltpu.roll(cur, 1, 0) + pltpu.roll(cur, rows - 1, 0))
            horizontal = ((own + (4.0 - CENTRE)) * cur - beside) * (2.0 / SPREAD)
            new = horizontal + (prod[:, 0:depth] + prod[:, depth : 2 * depth]) - prev
            basis[k + 2, pl.ds(x0, PLANES)] = new.reshape(PLANES, ez, depth)
            return inner_carry

        return lax.fori_loop(0, (ex - 2) // PLANES, planes, carry)

    lax.fori_loop(0, ITERS, grow, 0)

    pairs = [(i, j) for i in range(ITERS + 1) for j in range(i, ITERS + 1)]
    spot = {pair: k for k, pair in enumerate(pairs)}

    def gram_plane(x, sums):
        sums = list(sums)
        for z in range(0, cz, 8):
            vecs = [basis[k + 1, HX + x, HZ + z : HZ + z + 8, :] for k in range(ITERS + 1)]
            for q, (i, j) in enumerate(pairs):
                sums[q] = sums[q] + vecs[i] * vecs[j]
        return tuple(sums)

    sums = lax.fori_loop(
        0, cx, gram_plane, tuple(jnp.zeros((8, depth), F32) for unused in pairs)
    )
    lane = lax.broadcasted_iota(jnp.int32, (8, depth), 1)
    mine = jnp.zeros((8, depth), F32)
    for q, value in enumerate(sums):
        mine = mine + jnp.where(lane == q, jnp.sum(value, axis=1, keepdims=True), 0.0)
    mine = jnp.sum(mine, axis=0, keepdims=True)

    def all_bytes(ref, number, sem):
        there = ref.at[pl.ds(0, number)]
        return pltpu.make_async_copy(there, there, sem)

    def to_pair(ref, i):
        for s in range(1, n_gz):
            pltpu.make_async_remote_copy(
                src_ref=ref.at[gz],
                dst_ref=ref.at[gz],
                send_sem=group_send.at[i],
                recv_sem=group_recv.at[i],
                device_id=(gx, (gz + s) % n_gz, ta),
                device_id_type=MESH,
            ).start()

    def to_row(source, ref, i):
        def send(s, carry):
            there = (row + s) % trainers
            pltpu.make_async_remote_copy(
                src_ref=source(there),
                dst_ref=ref.at[row],
                send_sem=group_send.at[i],
                recv_sem=group_recv.at[i],
                device_id=in_row(there),
                device_id_type=MESH,
            ).start()
            return carry

        lax.fori_loop(1, trainers, send, 0)

    gram_pair[gz] = mine
    to_pair(gram_pair, 0)
    all_bytes(gram_pair, n_gz - 1, group_recv.at[0]).wait()
    gram_buf[row] = jnp.sum(gram_pair[...], axis=0)
    to_row(lambda there: gram_buf.at[row], gram_buf, 1)
    all_bytes(gram_buf, trainers - 1, group_recv.at[1]).wait()
    total = jnp.sum(gram_buf[...], axis=0)

    gram = {}
    for (i, j), q in spot.items():
        value = jnp.broadcast_to(total[0:1, q : q + 1], (8, depth))
        gram[i, j] = value
        gram[j, i] = value

    def inner(a, b):
        return tree_sum(
            a[i] * tree_sum(gram[i, j] * b[j] for j in range(len(b))) for i in range(len(a))
        )

    def operate(a):
        out = []
        for i in range(len(a) + 1):
            terms = []
            if i < len(a):
                terms.append(CENTRE * a[i])
            if i >= 1:
                terms.append((SPREAD / 2) * a[i - 1])
            if i + 1 < len(a):
                terms.append((SPREAD / 2) * a[i + 1])
            out.append(tree_sum(terms))
        return out

    one = jnp.ones((8, depth), F32)
    res, way, sol = [one], [one], []
    norm_now = gram[0, 0]
    for it in range(ITERS):
        applied = operate(way)
        step = norm_now / inner(way, applied)
        sol = [
            sol[i] + step * way[i] if i < len(sol) else step * way[i] for i in range(len(way))
        ]
        res = [
            res[i] - step * applied[i] if i < len(res) else -(step * applied[i])
            for i in range(len(applied))
        ]
        if it < ITERS - 1:
            norm_next = inner(res, res)
            ratio = norm_next / norm_now
            way = [res[i] + ratio * way[i] if i < len(way) else res[i] for i in range(len(res))]
            norm_now = norm_next

    def combine(coefs, x0):
        return tree_sum(
            coefs[k][None]
            * basis[k + 1, pl.ds(HX + x0, EL), HZ : HZ + cz, :].reshape(EL * cz // 8, 8, depth)
            for k in range(len(coefs))
        ).reshape(EL, cz, depth)

    def solve_planes(g, carry):
        field = combine(sol, g * EL)
        x_ref[pl.ds(g * EL, EL)] = field
        pooled[pl.ds(pl.multiple_of(g * cz, cz), cz), :] = jnp.sum(field, axis=0)
        return carry

    lax.fori_loop(0, cx // EL, solve_planes, 0)

    feat = (
        jnp.dot(
            pool_map, pooled[...], precision=lax.Precision.HIGHEST, preferred_element_type=F32
        )
        * (1.0 / EL)
    )
    shear = (feat[:, 1:2] - feat[:, 0:1]).astype(BF16)
    wall_feat = feat.astype(BF16)
    graph_mean = (dot_rows(links, wall_feat) * 0.25).astype(BF16)
    node_input = jnp.concatenate([wall_feat, graph_mean], axis=1)
    preact = jnp.dot(node_input, w_in_ref[...], preferred_element_type=F32)
    pre_sig = sigmoid(preact)
    hidden = (preact * pre_sig).astype(BF16)
    shears = jnp.broadcast_to(shear.astype(F32), (elements, depth)).astype(BF16)
    fwd_send[...] = (
        jnp.dot(
            place, jnp.concatenate([hidden, shears], axis=0), preferred_element_type=F32
        )
        .astype(BF16)
        .reshape(fwd_send.shape)
    )
    to_row(lambda there: fwd_send.at[there], fwd_buf, 2)
    fwd_buf[row] = fwd_send[row]

    def residual_planes(g, carry):
        r_ref[pl.ds(g * EL, EL)] = combine(res, g * EL)
        return carry

    lax.fori_loop(0, cx // EL, residual_planes, 0)

    all_bytes(fwd_buf, trainers - 1, group_recv.at[2]).wait()
    arrived = fwd_buf[...].astype(F32)
    slots = trainers * half
    hid = arrived[:, 0:half].reshape(slots, depth).astype(BF16)
    own_shear = arrived[:, half : 2 * half].reshape(slots, depth)[:, 0:1]
    own_head = head_ref[0]
    head_pre = jnp.dot(hid, own_head, preferred_element_type=F32)
    head_sig = sigmoid(head_pre)
    head_out = head_pre * head_sig
    w_out = w_out_ref[...]
    predicted = jnp.sum(head_out * w_out, axis=1, keepdims=True)
    misfit = (predicted - own_shear) * (1.0 / elements)
    out_part = jnp.sum(misfit * head_out, axis=0, keepdims=True)
    head_back = (
        misfit * w_out * (head_sig * (1.0 + head_pre * (1.0 - head_sig)))
    ).astype(BF16)
    back = dot_lanes(head_back, own_head).reshape(trainers, half, depth)
    out_hi = out_part.astype(BF16).astype(F32)
    out_lo = out_part - out_hi
    sub = lax.broadcasted_iota(jnp.int32, (half, depth), 0)
    out_rows = jnp.where(sub == 0, out_hi, jnp.where(sub == 1, out_lo, 0.0))
    ret_send[...] = jnp.concatenate(
        [back, jnp.broadcast_to(out_rows[None], (trainers, half, depth))], axis=1
    ).astype(BF16)
    to_row(lambda there: ret_send.at[there], ret_buf, 3)
    ret_buf[row] = ret_send[row]
    pair_heads[gz] = dot_rows(hid, head_back)
    to_pair(pair_heads, 4)
    slope = pre_sig * (1.0 + preact * (1.0 - pre_sig))

    all_bytes(ret_buf, trainers - 1, group_recv.at[3]).wait()
    returned = ret_buf[...]
    hidden_back = dot_rows(place_hidden, returned.reshape(trainers * 2 * half, depth))
    preact_back = (hidden_back * slope).astype(BF16)
    part = dot_rows(node_input, preact_back).astype(BF16)
    part_send[...] = part.reshape(part_send.shape)
    to_row(lambda there: part_send.at[there % chunks], part_buf, 5)
    part_buf[row] = part_send[row % chunks]
    out_plane = jnp.sum(returned[:, half : 2 * half].astype(F32), axis=0)

    all_bytes(part_buf, trainers - 1, group_recv.at[5]).wait()
    pair_sums[gz] = jnp.concatenate(
        [jnp.sum(part_buf[...].astype(F32), axis=0), out_plane], axis=0
    )
    to_pair(pair_sums, 6)
    all_bytes(pair_sums, n_gz - 1, group_recv.at[6]).wait()
    sums = jnp.sum(pair_sums[...], axis=0)

    if chunks == trainers:
        fin[row] = sums[0:chunk].astype(BF16)
        to_row(lambda there: fin.at[row], fin, 7)
    else:

        @pl.when(row < chunks)
        def own_chunk():
            fin[row] = sums[0:chunk].astype(BF16)
            to_row(lambda there: fin.at[row], fin, 7)

    og_ref[...] = sums[chunk : chunk + 1] + sums[chunk + 1 : chunk + 2]
    all_bytes(pair_heads, n_gz - 1, group_recv.at[4]).wait()
    hg_ref[0] = jnp.sum(pair_heads[...], axis=0)

    for copy in x_copies + z_copies + corners:
        copy.wait_send()
    for ref, number, i in (
        (gram_pair, n_gz, 0),
        (gram_buf, trainers, 1),
        (fwd_buf, trainers, 2),
        (ret_buf, trainers, 3),
        (pair_heads, n_gz, 4),
        (part_buf, trainers, 5),
        (pair_sums, n_gz, 6),
    ):
        all_bytes(ref, number - 1, group_send.at[i]).wait()

    if chunks == trainers:
        all_bytes(fin, trainers - 1, group_recv.at[7]).wait()
        all_bytes(fin, trainers - 1, group_send.at[7]).wait()
    else:

        @pl.when(row < chunks)
        def owner_waits():
            all_bytes(fin, chunks - 1, group_recv.at[7]).wait()

            def one_send(s, carry):
                pltpu.make_async_copy(fin.at[row], fin.at[row], group_send.at[7]).wait()
                return carry

            lax.fori_loop(1, trainers, one_send, 0)

        @pl.when(row >= chunks)
        def others_wait():
            all_bytes(fin, chunks, group_recv.at[7]).wait()

    ig_ref[...] = fin[...].astype(F32).reshape(ig_ref.shape)


def hand_over(*refs):
    count = (len(refs) - 2) // 3
    load_sem, store_sem = refs[-2:]
    loads, stores = [], []
    for i in range(count):
        source, target, held = refs[i], refs[count + i], refs[2 * count + i]
        loads.append(pltpu.make_async_copy(source, held, load_sem.at[i]))
        stores.append(pltpu.make_async_copy(held, target, store_sem.at[i]))
    for load in loads:
        load.start()
    for load, store in zip(loads, stores):
        load.wait()
        store.start()
    for store in stores:
        store.wait()


def local(
    sizes,
    right_side,
    diagonal,
    coupling,
    wall_owner,
    neighbours,
    input_weight,
    head_weights,
    output_weight,
):
    n_gx, n_gz, n_ta = sizes
    trainers = n_gx * n_ta
    cx, cz, depth = right_side.shape
    ex, ez = cx + 2 * HX, cz + 2 * HZ
    elements = wall_owner.shape[0]
    capacity = max(2, 2 * elements // trainers)
    half = -(-capacity // 8) * 8
    wide = input_weight.shape[0]
    chunks = min(trainers, wide // 16)
    chunk = wide // chunks
    vmem = pl.BlockSpec(memory_space=pltpu.VMEM)
    hbm = pl.BlockSpec(memory_space=pl.ANY)
    dma = pltpu.SemaphoreType.DMA
    rows = (trainers, 2 * half, depth)
    shapes = (
        jax.ShapeDtypeStruct(right_side.shape, F32),
        jax.ShapeDtypeStruct(right_side.shape, F32),
        jax.ShapeDtypeStruct((wide, depth), F32),
        jax.ShapeDtypeStruct((1, depth, depth), F32),
        jax.ShapeDtypeStruct((1, depth), F32),
    )
    results = pl.pallas_call(
        functools.partial(kernel, sizes),
        out_shape=shapes,
        in_specs=[hbm] * 8,
        out_specs=(vmem,) * 5,
        scratch_shapes=[
            pltpu.VMEM((ITERS + 2, ex, ez, depth), F32),
            pltpu.VMEM((ex, ez, depth), F32),
            pltpu.VMEM((depth, depth), F32),
            pltpu.VMEM((1, elements), jnp.int32),
            pltpu.VMEM((neighbours.shape[1], elements), jnp.int32),
            pltpu.VMEM((wide, depth), BF16),
            pltpu.VMEM((1, depth, depth), BF16),
            pltpu.VMEM((1, depth), F32),
            pltpu.VMEM((2 * depth, 2 * depth), BF16),
            pltpu.VMEM((n_gz, 1, depth), F32),
            pltpu.VMEM((trainers, 1, depth), F32),
            pltpu.VMEM((elements * EL, depth), F32),
            pltpu.VMEM(rows, BF16),
            pltpu.VMEM(rows, BF16),
            pltpu.VMEM(rows, BF16),
            pltpu.VMEM(rows, BF16),
            pltpu.VMEM((chunks, chunk, depth), BF16),
            pltpu.VMEM((trainers, chunk, depth), BF16),
            pltpu.VMEM((n_gz, depth, depth), F32),
            pltpu.VMEM((n_gz, chunk + half, depth), F32),
            pltpu.VMEM((chunks, chunk, depth), BF16),
            dma((8,)),
            dma((8,)),
            dma((8,)),
            dma((8,)),
            dma((8,)),
            dma((8,)),
            dma((8,)),
        ],
        compiler_params=pltpu.CompilerParams(
            collective_id=0, has_side_effects=True, vmem_limit_bytes=56 * 1024 * 1024
        ),
    )(
        right_side,
        diagonal,
        coupling,
        wall_owner.reshape(1, -1),
        neighbours.T,
        input_weight,
        head_weights,
        output_weight.reshape(1, -1),
    )
    field, residual, input_grad, head_grad, output_grad = pl.pallas_call(
        hand_over,
        out_shape=shapes,
        in_specs=[hbm] * 5,
        out_specs=(hbm,) * 5,
        scratch_shapes=[pltpu.VMEM(s.shape, s.dtype) for s in shapes] + [dma((5,)), dma((5,))],
    )(*results)
    return (field, residual, input_grad, head_grad, output_grad.reshape(-1))


def solution(mesh):
    placed = (
        P(("gx", "ta"), "gz", None),
        P(("gx", "ta"), "gz", None),
        P(),
        P(("gx", "gz", "ta"), None),
        P(("gx", "gz", "ta"), None),
        P(),
        P(("gx", "ta"), None, None),
        P(),
    )
    sizes = tuple(mesh.shape[name] for name in ("gx", "gz", "ta"))
    return jax.shard_map(
        functools.partial(local, sizes),
        mesh=mesh,
        in_specs=placed,
        out_specs=(
            P(("gx", "ta"), "gz", None),
            P(("gx", "ta"), "gz", None),
            P(),
            P(("gx", "ta"), None, None),
            P(),
        ),
        check_vma=False,
    )
```
